32 devices in a mesh: fsdp: 4 (over z), seq: 8 (over y, x, core).
Axes of the slice: x: 2, y: 2, z: 4, core: 2. Of those that a mesh axis runs over, the one named last changes fastest.
Arguments:
- tokens: bfloat16 [4, 1024, 1024], P('fsdp', 'seq'), may hold values from -6 to 6
- segment_ids: int32 [4, 1024], P('fsdp'), may hold values from 0 to 2, as said below
- w_qkv: bfloat16 [1024, 3072], P('fsdp'), may hold values from -0.1875 to 0.1875
- w_attn_out: bfloat16 [1024, 1024], P('fsdp'), may hold values from -1.25 to 1.25
- w_in: bfloat16 [1024, 2, 2624], P('fsdp'), may hold values from -0.1875 to 0.1875
- w_mlp_out: bfloat16 [2624, 1024], P(None, 'fsdp'), may hold values from -0.125 to 0.125
- norm_gains: bfloat16 [2, 1024], P(None, 'fsdp'), may hold values from 0.5 to 1.5
- cotangent: bfloat16 [4, 1024, 1024], P('fsdp', 'seq'), may hold values from -6 to 6
Outputs:
- outputs: bfloat16 [4, 1024, 1024], P('fsdp', 'seq')
- input_grad: float32 [4, 1024, 1024], P('fsdp', 'seq')
- grad_w_qkv: float32 [1024, 3072], P(('fsdp', 'seq'))
- grad_w_attn_out: float32 [1024, 1024], P(('fsdp', 'seq'))
- grad_w_in: float32 [1024, 2, 2624], P(('fsdp', 'seq'))
- grad_w_mlp_out: float32 [2624, 1024], P(None, ('fsdp', 'seq'))
- grad_norm_gains: float32 [2, 1024], P(None, ('fsdp', 'seq'))
The draws below stay inside these ranges and needn't reach their ends.
Inputs may be any that keep to these rules, and one draw needn't show every extreme that they name: `segment_ids`: each sequence holds at most three documents, numbered from 0 in order, so ids never fall along a sequence. No document boundary lies within 256 tokens of a sequence's ends or within 128 tokens of its middle.
All inputs are finite; a program needn't handle non-finite values.
Results may differ from the reference program's by a relative error of at most 0.014.
Values may be sent and summed in bfloat16 or wider, within the bound.
A program may use at most 256 MiB of HBM per device.

```python
import math
import jax
import jax.numpy as jnp
from jax import lax

D = 1024
HEADS = 16
HD = 64
FF = 2624
WIN = 128
TOK_DEV = 128
L = 1024
ROWS = 4


def draw_segment_ids(key, part):
    key = jax.random.fold_in(key, 11)
    key_one, key_two, key_three = jax.random.split(key, 3)
    first_cut = jax.random.randint(key_one, (ROWS, 1), 2 * TOK_DEV, L // 2 - TOK_DEV)
    second_cut = jax.random.randint(key_two, (ROWS, 1), L // 2 + TOK_DEV, L - 2 * TOK_DEV)
    whole_row = jax.random.randint(key_three, (), 0, ROWS)
    row_index = jnp.arange(ROWS, dtype=jnp.int32)[:, None]
    first_cut = jnp.where(row_index == whole_row, L, first_cut)
    second_cut = jnp.where(row_index == whole_row, L, second_cut)
    position = jnp.arange(L, dtype=jnp.int32)[None, :]
    return (position >= first_cut).astype(jnp.int32) + (position >= second_cut).astype(jnp.int32)


def block_levels(stream_key, extent, shards, least, largest):
    def one(axis_at, shards_of):
        heights = jax.random.uniform(jax.random.fold_in(jax.random.fold_in(stream_key, 6), axis_at), (shards_of,), jnp.float32, least / len(shards), largest / len(shards))
        return jnp.repeat(jnp.exp(heights), extent[axis_at] // shards_of).reshape((-1,) + (1,) * (len(extent) - axis_at - 1))

    loudness = one(*shards[0])
    for cut in shards[1:]:
        loudness = loudness * one(*cut)
    return loudness


def gaussian(rng, extent, scale, limit, cuts=(), kind=jnp.bfloat16):
    values = scale * jax.random.normal(rng, extent, jnp.float32)
    if cuts:
        values = values * block_levels(rng, extent, cuts, -0.22, 0.18)
    return jnp.clip(values, -limit, limit).astype(kind)


def setup_inputs(seed: int = 0) -> dict:
    keys = jax.random.split(jax.random.key(seed), 9)
    tokens = gaussian(keys[0], (ROWS, L, D), 1.0, 6.0, ((0, 4), (1, 8)))
    segment_ids = draw_segment_ids(jax.random.fold_in(keys[8], 71), 0)
    w_qkv = gaussian(keys[2], (D, 3 * D), D ** -0.5, 0.1875, ((0, 4),))
    w_attn_out = gaussian(keys[3], (D, D), (3 * D // WIN) ** -0.5, 1.25, ((0, 4),))
    w_in = gaussian(keys[4], (D, 2, FF), D ** -0.5, 0.1875, ((0, 4),))
    w_mlp_out = gaussian(keys[5], (FF, D), FF ** -0.5, 0.125, ((1, 4),))
    norm_gains = jnp.clip(1.0 + 0.1 * jax.random.normal(keys[6], (2, D), jnp.float32), 0.5, 1.5).astype(jnp.bfloat16)
    cotangent = gaussian(keys[7], (ROWS, L, D), 1.0, 6.0, ((0, 4), (1, 8)))
    return {"tokens": tokens, "segment_ids": segment_ids, "w_qkv": w_qkv, "w_attn_out": w_attn_out, "w_in": w_in, "w_mlp_out": w_mlp_out, "norm_gains": norm_gains, "cotangent": cotangent}


@jax.custom_vjp
def low(v):
    return lax.optimization_barrier(v.astype(jnp.bfloat16)).astype(jnp.float32)

@jax.custom_vjp
def low_back(v):
    return v

def low_keep(v):
    return (low(v), None)

def low_pass(kept, grad):
    return (grad,)

def back_keep(v):
    return (v, None)

def back_low(kept, grad):
    return (low(grad),)
low.defvjp(low_keep, low_pass)
low_back.defvjp(back_keep, back_low)
norm_eps = 1e-05
rope_base = 10000.0
masked_score = -1e+30
highest = lax.Precision.HIGHEST

def layer_norm(values, norm_gain):
    centre = values - lax.optimization_barrier(jnp.mean(values, axis=-1, keepdims=True))
    spread = lax.optimization_barrier(jnp.mean(centre * centre, axis=-1, keepdims=True))
    return centre * lax.rsqrt(spread + norm_eps) * norm_gain

def rope_tables(positions, head_dim):
    half_dim = head_dim // 2
    inv_freq = rope_base ** (-(2.0 * jnp.arange(half_dim, dtype=jnp.float32)) / head_dim)
    angles = positions.astype(jnp.float32)[:, None] * inv_freq[None, :]
    return (jnp.cos(angles), jnp.sin(angles))

def rotate(values, cos_table, sin_table, head_count):
    tok_rows = values.shape[0]
    shaped = values.reshape(tok_rows, head_count, -1)
    half_dim = shaped.shape[-1] // 2
    first_half = shaped[..., :half_dim]
    second = shaped[..., half_dim:]
    cos_part = cos_table[:, None, :]
    sin_part = sin_table[:, None, :]
    turned = jnp.concatenate([first_half * cos_part - second * sin_part, second * cos_part + first_half * sin_part], axis=-1)
    return turned.reshape(tok_rows, -1)

def attend(query_rows, key_rows, value_rows, row_ids):
    length = query_rows.shape[0]
    half_win = WIN // 2
    block_rows = math.gcd(length, 512)
    score_scale = HD ** (-0.5)
    key_pad = jnp.pad(key_rows, ((half_win, half_win), (0, 0)))
    value_pad = jnp.pad(value_rows, ((half_win, half_win), (0, 0)))
    ids_pad = jnp.pad(row_ids, (half_win, half_win), constant_values=-1)

    @jax.checkpoint
    def one_block(block_index):
        block_start = (block_index * block_rows).astype(jnp.int32)
        q_rows = lax.dynamic_slice_in_dim(query_rows, block_start, block_rows).reshape(block_rows, HEADS, HD)
        k_rows = lax.dynamic_slice_in_dim(key_pad, block_start, block_rows + 2 * half_win).reshape(-1, HEADS, HD)
        v_rows = lax.dynamic_slice_in_dim(value_pad, block_start, block_rows + 2 * half_win).reshape(-1, HEADS, HD)
        q_ids = lax.dynamic_slice_in_dim(row_ids, block_start, block_rows)
        k_ids = lax.dynamic_slice_in_dim(ids_pad, block_start, block_rows + 2 * half_win)
        offsets = jnp.arange(block_rows)[:, None] - jnp.arange(block_rows + 2 * half_win)[None, :] + half_win
        allowed = (jnp.abs(offsets) <= half_win) & (q_ids[:, None] == k_ids[None, :])
        scores = low_back(jnp.einsum('thd,shd->hts', q_rows, k_rows, precision=highest) * score_scale)
        scores = jnp.where(allowed[None], scores, masked_score)
        row_max = lax.optimization_barrier(jnp.max(scores, axis=-1, keepdims=True))
        exponent = jnp.exp(scores - row_max)
        attn_prob = exponent / lax.optimization_barrier(jnp.sum(exponent, axis=-1, keepdims=True))
        result = jnp.einsum('hts,shd->thd', low(attn_prob), v_rows, precision=highest)
        return result.reshape(block_rows, D)
    blocks = lax.map(one_block, jnp.arange(length // block_rows, dtype=jnp.int32))
    return blocks.reshape(length, D)

def forward_row(x_row, row_ids, qkv_weight, attn_weight, in_weight, mlp_weight, gain_pair):
    length = x_row.shape[0]
    cos_table, sin_table = rope_tables(jnp.arange(length, dtype=jnp.int32), HD)
    a_one = low(layer_norm(x_row, gain_pair[0]))
    qkv_full = low_back(jnp.dot(a_one, qkv_weight, preferred_element_type=jnp.float32, precision=highest))
    query_rows = low(rotate(qkv_full[:, :D], cos_table, sin_table, HEADS))
    key_rows = low(rotate(qkv_full[:, D:2 * D], cos_table, sin_table, HEADS))
    value_rows = low(qkv_full[:, 2 * D:])
    attn_o = low(low_back(attend(query_rows, key_rows, value_rows, row_ids)))
    branch = low_back(jnp.dot(attn_o, attn_weight, preferred_element_type=jnp.float32, precision=highest))
    residual = x_row + branch
    a_two = low(layer_norm(residual, gain_pair[1]))
    upward = low_back(jnp.einsum('td,dcf->tcf', a_two, in_weight, precision=highest))
    middle = low(jax.nn.gelu(upward[:, 0], approximate=False) * upward[:, 1])
    mlp_part = low_back(jnp.dot(middle, mlp_weight, preferred_element_type=jnp.float32, precision=highest))
    return residual + mlp_part

def reference(tokens, segment_ids, w_qkv, w_attn_out, w_in, w_mlp_out, norm_gains, cotangent):

    def forward(inputs, qkv_weight, attn_weight, in_weight, mlp_weight, gain_pair):
        row_layer = jax.checkpoint(lambda x_row, row_ids: forward_row(x_row, row_ids, qkv_weight, attn_weight, in_weight, mlp_weight, gain_pair))

        def row_step(row_carry, row_pair):
            return (row_carry, row_layer(row_pair[0], row_pair[1]))
        _, results = lax.scan(row_step, jnp.zeros((), jnp.float32), (inputs, segment_ids))
        return results
    params = (tokens.astype(jnp.float32), w_qkv.astype(jnp.float32), w_attn_out.astype(jnp.float32), w_in.astype(jnp.float32), w_mlp_out.astype(jnp.float32), norm_gains.astype(jnp.float32))
    results, pullback = jax.vjp(forward, *params)
    gradients = pullback(cotangent.astype(jnp.float32))
    return (results.astype(jnp.bfloat16), gradients[0], gradients[1], gradients[2], gradients[3], gradients[4], gradients[5])
```

```python
import functools

import jax
import jax.numpy as jnp
from jax import lax
from jax.experimental import pallas as pl
from jax.experimental.pallas import tpu as pltpu
from jax.sharding import PartitionSpec as P

HEADS = 16
HD = 64
WIN = 128


norm_eps = 1e-05
rope_base = 10000.0
masked_score = -1e30
MESH = pl.DeviceIdType.MESH
LANE = 1024
SUB = 256


def up_to(size, unit):
    return -(-size // unit) * unit


def gather_kernel(n, count, *refs):
    ins, outs = refs[:count], refs[count : 2 * count]
    z_send, z_recv, one_send, one_recv, two_send, two_recv, core_send, core_recv, own_sem = refs[
        2 * count :
    ]
    me = lax.axis_index("fsdp")
    spot = lax.axis_index("seq")
    core = lax.rem(spot, 2)
    bit_x = lax.rem(spot // 2, 2)
    bit_y = lax.rem(spot // 4, 2)
    part = bit_y * 4 + bit_x * 2 + core
    base = spot - part
    height = ins[0].shape[0]
    block = height // 8

    def flip(number, mask):
        c = number % 2
        x = (number // 2) % 2
        y = number // 4
        c = 1 - c if mask & 1 else c
        x = 1 - x if mask & 2 else x
        y = 1 - y if mask & 4 else y
        return y * 4 + x * 2 + c

    mates = {mask: base + flip(part, mask) for mask in (1, 2, 4)}

    barrier = pltpu.get_barrier_semaphore()

    def greet(target):
        pl.semaphore_signal(barrier, inc=1, device_id=target, device_id_type=MESH)

    for mask in (1, 2, 4):
        greet((me, mates[mask]))

    @pl.when(me > 0)
    def _():
        greet((me - 1, spot))

    @pl.when(me < n - 1)
    def _():
        greet((me + 1, spot))

    peers = 3 + jnp.where(me > 0, 1, 0) + jnp.where(me < n - 1, 1, 0)
    pl.semaphore_wait(barrier, peers)

    def region(k, origin, mask):
        start = pl.multiple_of(origin * height + flip(part, mask) * block, block)
        return outs[k].at[pl.ds(start, block)]

    def remote(src, dst, send, recv, target):
        return pltpu.make_async_remote_copy(
            src_ref=src, dst_ref=dst, send_sem=send, recv_sem=recv, device_id=target, device_id_type=MESH
        )

    def z_copy(way, origin, k, own=False):
        if own:
            src = ins[k].at[pl.ds(pl.multiple_of(part * block, block), block)]
        else:
            src = region(k, origin, 0)
        target = me + 1 if way == 0 else me - 1
        return remote(
            src, region(k, origin, 0), z_send.at[way, origin, k], z_recv.at[origin, k], (target, spot)
        )

    def firsts(k):
        return (2, 4) if k % 2 == 0 else (4, 2)

    def one_copy(origin, k, mask=0):
        place = region(k, origin, mask)
        return remote(
            place, place, one_send.at[origin, k], one_recv.at[origin, k], (me, mates[firsts(k)[0]])
        )

    def two_copy(origin, k, index, mask):
        place = region(k, origin, mask)
        return remote(
            place,
            place,
            two_send.at[origin, k, index],
            two_recv.at[origin, k, index],
            (me, mates[firsts(k)[1]]),
        )

    def core_copy(origin, k, index, mask):
        place = region(k, origin, mask)
        return remote(
            place,
            place,
            core_send.at[origin, k, index],
            core_recv.at[origin, k, index],
            (me, mates[1]),
        )

    def can_go(way):
        return me < n - 1 if way == 0 else me > 0

    def has(way, d):
        return me >= d if way == 0 else me + d <= n - 1

    for k in range(count):
        for way in (0, 1):

            @pl.when(can_go(way))
            def _(k=k, way=way):
                z_copy(way, me, k, own=True).start()

    def own_copy(k):
        rows = pl.ds(pl.multiple_of(me * height, height), height)
        return pltpu.make_async_copy(ins[k], outs[k].at[rows], own_sem.at[k])

    for k in range(count):
        own_copy(k).start()

    def came(way, d, k):
        origin = me - d if way == 0 else me + d

        @pl.when(has(way, d))
        def _():
            z_copy(way, origin, k).wait_recv()

            @pl.when(can_go(way))
            def _():
                z_copy(way, origin, k).start()

            one_copy(origin, k).start()
            two_copy(origin, k, 0, 0).start()
            core_copy(origin, k, 0, 0).start()

    def second(way, d, k):
        origin = me - d if way == 0 else me + d
        m_one, m_two = firsts(k)

        @pl.when(has(way, d))
        def _():
            one_copy(origin, k, m_one).wait_recv()
            two_copy(origin, k, 1, m_one).start()
            core_copy(origin, k, 1, m_one).start()

    def third(way, d, k):
        origin = me - d if way == 0 else me + d
        m_one, m_two = firsts(k)

        @pl.when(has(way, d))
        def _():
            two_copy(origin, k, 0, m_two).wait_recv()
            core_copy(origin, k, 2, m_two).start()
            two_copy(origin, k, 1, m_one + m_two).wait_recv()
            core_copy(origin, k, 3, m_one + m_two).start()

    def last(way, d, k):
        origin = me - d if way == 0 else me + d
        m_one, m_two = firsts(k)
        masks = (0, m_one, m_two, m_one + m_two)

        @pl.when(has(way, d))
        def _():
            for index, mask in enumerate(masks):
                core_copy(origin, k, index, mask + 1).wait_recv()
                core_copy(origin, k, index, mask).wait_send()
            one_copy(origin, k).wait_send()
            two_copy(origin, k, 0, 0).wait_send()
            two_copy(origin, k, 1, m_one).wait_send()

            @pl.when(can_go(way))
            def _():
                z_copy(way, origin, k).wait_send()

    steps = [(way, d, k) for d in range(1, n) for k in range(count) for way in (0, 1)]
    lag = 4
    total = len(steps)
    for i in range(total + 2 * lag):
        if i < total:
            came(*steps[i])
        if 0 <= i - lag < total:
            second(*steps[i - lag])
        if 0 <= i - 2 * lag < total:
            third(*steps[i - 2 * lag])
    for step in steps:
        last(*step)
    for k in range(count):
        for way in (0, 1):

            @pl.when(can_go(way))
            def _(k=k, way=way):
                z_copy(way, me, k, own=True).wait_send()

        own_copy(k).wait()


def gather_weights(shards):
    n = lax.axis_size("fsdp")
    count = len(shards)
    sem = pltpu.SemaphoreType.DMA
    return pl.pallas_call(
        functools.partial(gather_kernel, n, count),
        out_shape=[jax.ShapeDtypeStruct((n * s.shape[0], s.shape[1]), s.dtype) for s in shards],
        in_specs=[pl.BlockSpec(memory_space=pl.ANY)] * count,
        out_specs=[pl.BlockSpec(memory_space=pl.ANY)] * count,
        scratch_shapes=[
            sem((2, n, count)),
            sem((n, count)),
            sem((n, count)),
            sem((n, count)),
            sem((n, count, 2)),
            sem((n, count, 2)),
            sem((n, count, 4)),
            sem((n, count, 4)),
            sem((count,)),
        ],
        compiler_params=pltpu.CompilerParams(collective_id=0, has_side_effects=True),
        name="gather_weights",
    )(*shards)


def scatter_kernel(
    n, edges, at_ref, b_ref, gcol_ref, out_ref,
    gbuf, r_core, r_one, r_two, r_z,
    core_send, core_recv, one_send, one_recv, two_send, two_recv, z_send, z_recv,
):
    me = lax.axis_index("fsdp")
    spot = lax.axis_index("seq")
    c = lax.rem(spot, 2)
    x = lax.rem(spot // 2, 2)
    y = spot // 4
    r = gbuf.shape[5]
    chunks = gbuf.shape[0]
    units = chunks // 2
    mate_c = y * 4 + x * 2 + (1 - c)
    mate_x = y * 4 + (1 - x) * 2 + c
    mate_y = (1 - y) * 4 + x * 2 + c

    barrier = pltpu.get_barrier_semaphore()
    for mate in (mate_c, mate_x, mate_y):
        pl.semaphore_signal(barrier, inc=1, device_id=(me, mate), device_id_type=MESH)
    for d in range(1, n):
        pl.semaphore_signal(
            barrier, inc=1, device_id=(lax.rem(me + d, n), spot), device_id_type=MESH
        )
    pl.semaphore_wait(barrier, 3 + n - 1)

    def remote(src, dst, send, recv, target):
        return pltpu.make_async_remote_copy(
            src_ref=src, dst_ref=dst, send_sem=send, recv_sem=recv, device_id=target, device_id_type=MESH
        )

    def core_copy(j):
        return remote(
            gbuf.at[j, :, :, :, 1 - c], r_core.at[j], core_send.at[j], core_recv.at[j], (me, mate_c)
        )

    def one_copy(j, e):
        src = gbuf.at[j, :, :, 1 - x, c] if e == 0 else gbuf.at[j, :, 1 - y, :, c]
        mate = mate_x if e == 0 else mate_y
        return remote(src, r_one.at[j], one_send.at[j], one_recv.at[j], (me, mate))

    def two_copy(j, e):
        src = gbuf.at[j, :, 1 - y, x, c] if e == 0 else gbuf.at[j, :, y, 1 - x, c]
        mate = mate_y if e == 0 else mate_x
        return remote(src, r_two.at[j], two_send.at[j], two_recv.at[j], (me, mate))

    def z_copy(j, d):
        other = lax.rem(me + d, n)
        return remote(
            gbuf.at[j, other, y, x, c],
            r_z.at[j, d - 1],
            z_send.at[j, d - 1],
            z_recv.at[j, d - 1],
            (other, spot),
        )

    def plus(left, right):
        return (left.astype(jnp.float32) + right.astype(jnp.float32)).astype(left.dtype)

    def make(k):
        def one_tile(u, carry):
            t = k * (2 * LANE // SUB) + u
            which = jnp.int32(0)
            for edge in edges:
                which = which + jnp.where(t >= edge, 1, 0).astype(jnp.int32)
            columns = pl.ds(pl.multiple_of(t * SUB, SUB), SUB)
            value = jnp.dot(at_ref[which], b_ref[:, columns], preferred_element_type=jnp.float32)
            value = value.astype(gbuf.dtype).reshape(gbuf.shape[1:6] + (SUB,))
            j = k * 2 + u // (LANE // SUB)
            inner = pl.ds(pl.multiple_of((u % (LANE // SUB)) * SUB, SUB), SUB)
            gbuf[j, :, :, :, :, :, inner] = value
            return carry

        lax.fori_loop(0, 2 * LANE // SUB, one_tile, 0)

    def turn(it, carry):
        @pl.when(it < units)
        def _():
            make(it)

            @pl.when(it == units - 1)
            def _():
                wide = gcol_ref.shape[1]
                gbuf[chunks - 1, :, :, :, :, :, LANE - wide :] = gcol_ref[...].reshape(
                    gbuf.shape[1:6] + (wide,)
                )

            core_copy(2 * it).start()
            core_copy(2 * it + 1).start()

        @pl.when((it >= 1) & (it < units + 1))
        def _():
            for e in (0, 1):
                j = 2 * (it - 1) + e
                core_copy(j).wait()
                for i in range(n):
                    for a in (0, 1):
                        gbuf[j, i, a, :, c] = plus(gbuf[j, i, a, :, c], r_core[j, i, a])
                one_copy(j, e).start()

        @pl.when((it >= 2) & (it < units + 2))
        def _():
            for e in (0, 1):
                j = 2 * (it - 2) + e
                one_copy(j, e).wait()
                for i in range(n):
                    if e == 0:
                        gbuf[j, i, :, x, c] = plus(gbuf[j, i, :, x, c], r_one[j, i])
                    else:
                        gbuf[j, i, y, :, c] = plus(gbuf[j, i, y, :, c], r_one[j, i])
                two_copy(j, e).start()

        @pl.when((it >= 3) & (it < units + 3))
        def _():
            for e in (0, 1):
                j = 2 * (it - 3) + e
                two_copy(j, e).wait()
                for i in range(n):
                    gbuf[j, i, y, x, c] = plus(gbuf[j, i, y, x, c], r_two[j, i])
                for d in range(1, n):
                    z_copy(j, d).start()

        @pl.when(it >= 4)
        def _():
            for e in (0, 1):
                j = 2 * (it - 4) + e
                total = gbuf[j, me, y, x, c].astype(jnp.float32)
                for d in range(1, n):
                    z_copy(j, d).wait()
                    total = total + r_z[j, d - 1].astype(jnp.float32)
                out_ref[:, pl.ds(pl.multiple_of(j * LANE, LANE), LANE)] = total

        return carry

    lax.fori_loop(0, units + 4, turn, 0)


def scatter_sums(lefts, rights, gain_columns, edges):
    n = lax.axis_size("fsdp")
    rows = lefts.shape[1]
    r = rows // (8 * n)
    width = rights.shape[1]
    chunks = width // LANE
    half = jnp.bfloat16
    sem = pltpu.SemaphoreType.DMA
    vmem = pl.BlockSpec(memory_space=pltpu.VMEM)
    return pl.pallas_call(
        functools.partial(scatter_kernel, n, edges),
        out_shape=jax.ShapeDtypeStruct((r, width), jnp.float32),
        in_specs=[vmem] * 3,
        out_specs=vmem,
        scratch_shapes=[
            pltpu.VMEM((chunks, n, 2, 2, 2, r, LANE), half),
            pltpu.VMEM((chunks, n, 2, 2, r, LANE), half),
            pltpu.VMEM((chunks, n, 2, r, LANE), half),
            pltpu.VMEM((chunks, n, r, LANE), half),
            pltpu.VMEM((chunks, n - 1, r, LANE), half),
            sem((chunks,)),
            sem((chunks,)),
            sem((chunks,)),
            sem((chunks,)),
            sem((chunks,)),
            sem((chunks,)),
            sem((chunks, n - 1)),
            sem((chunks, n - 1)),
        ],
        compiler_params=pltpu.CompilerParams(
            collective_id=1, has_side_effects=True, vmem_limit_bytes=62 * 1024 * 1024
        ),
        name="scatter_sums",
    )(lefts, rights, gain_columns)


def padded(cells, sides, width):
    for axis, dim in sides:
        count = lax.axis_size(axis)
        ends = count - 1
        head = lax.slice_in_dim(cells, 0, width, axis=dim)
        tail = lax.slice_in_dim(cells, cells.shape[dim] - width, cells.shape[dim], axis=dim)
        cells = jnp.concatenate(
            [
                lax.ppermute(tail, axis, [(i, (i + 1) % count) for i in range(ends)]),
                cells,
                lax.ppermute(head, axis, [((i + 1) % count, i) for i in range(ends)]),
            ],
            axis=dim,
        )
    return cells


def layer_norm(values, norm_gain):
    centre = values - jnp.mean(values, axis=-1, keepdims=True)
    spread = jnp.mean(centre * centre, axis=-1, keepdims=True)
    return centre * lax.rsqrt(spread + norm_eps) * norm_gain


def rope_tables(positions, head_dim):
    half_dim = head_dim // 2
    inv_freq = rope_base ** (-(2.0 * jnp.arange(half_dim, dtype=jnp.float32)) / head_dim)
    angles = positions.astype(jnp.float32)[:, None] * inv_freq[None, :]
    return (jnp.cos(angles), jnp.sin(angles))


def rotate(values, cos_table, sin_table, head_count):
    tok_rows = values.shape[0]
    shaped = values.reshape(tok_rows, head_count, -1)
    half_dim = shaped.shape[-1] // 2
    first_half = shaped[..., :half_dim]
    second = shaped[..., half_dim:]
    cos_part = cos_table[:, None, :]
    sin_part = sin_table[:, None, :]
    turned = jnp.concatenate(
        [first_half * cos_part - second * sin_part, second * cos_part + first_half * sin_part],
        axis=-1,
    )
    return turned.reshape(tok_rows, -1)


def gated_gelu(gate, linear):
    return jax.nn.gelu(gate, approximate=False) * linear


def local(tokens, segment_ids, w_qkv, w_attn_out, w_in, w_mlp_out, norm_gains, cotangent):
    tok_rows = tokens.shape[1]
    model_width = tokens.shape[2]
    half_win = WIN // 2
    score_scale = HD ** (-0.5)
    row_start = lax.axis_index("seq") * tok_rows
    ff = w_in.shape[2]
    ff_wide = up_to(ff, 128)
    tail = up_to(ff_wide + 128, SUB) - ff_wide
    stretch = ((0, 0), (0, ff_wide - ff))
    full_qkv, full_out, full_gate, full_lin, full_down = gather_weights(
        [
            w_qkv,
            w_attn_out,
            jnp.pad(w_in[:, 0], stretch),
            jnp.pad(w_in[:, 1], stretch),
            jnp.concatenate(
                [
                    jnp.pad(w_mlp_out.T, stretch),
                    jnp.pad(norm_gains.T, ((0, 0), (0, tail - norm_gains.shape[0]))),
                ],
                axis=1,
            ),
        ]
    )
    full_mlp = full_down[:, :ff_wide]
    gain_pair = full_down[:, ff_wide : ff_wide + norm_gains.shape[0]].T.astype(jnp.float32)
    inputs = tokens[0].astype(jnp.float32)
    cos_table, sin_table = rope_tables(row_start + jnp.arange(tok_rows, dtype=jnp.int32), HD)
    h_one, norm_one_back = jax.vjp(layer_norm, inputs, gain_pair[0])
    a_one = h_one.astype(jnp.bfloat16)
    qkv_full = jnp.dot(a_one, full_qkv, preferred_element_type=jnp.float32)
    query_rows = rotate(qkv_full[:, :model_width], cos_table, sin_table, HEADS).astype(jnp.bfloat16)
    key_rows = rotate(
        qkv_full[:, model_width : 2 * model_width], cos_table, sin_table, HEADS
    ).astype(jnp.bfloat16)
    value_rows = qkv_full[:, 2 * model_width :].astype(jnp.bfloat16)
    kv_wide = padded(jnp.concatenate([key_rows, value_rows], axis=1), (("seq", 0),), half_win)
    key_wide = kv_wide[:, :model_width].reshape(-1, HEADS, HD)
    value_wide = kv_wide[:, model_width:].reshape(-1, HEADS, HD)
    row_ids = segment_ids[0]
    ids_pad = jnp.pad(row_ids, (half_win, half_win), constant_values=-1)
    k_ids = lax.dynamic_slice_in_dim(ids_pad, row_start, tok_rows + 2 * half_win)
    q_ids = lax.dynamic_slice_in_dim(row_ids, row_start, tok_rows)
    offsets = (
        jnp.arange(tok_rows)[:, None] - jnp.arange(tok_rows + 2 * half_win)[None, :] + half_win
    )
    allowed = (jnp.abs(offsets) <= half_win) & (q_ids[:, None] == k_ids[None, :])
    q_heads = query_rows.reshape(tok_rows, HEADS, HD)
    scores = (
        jnp.einsum("thd,shd->hts", q_heads, key_wide, preferred_element_type=jnp.float32)
        * score_scale
    )
    scores = jnp.where(allowed[None], scores, masked_score)
    row_max = jnp.max(scores, axis=-1, keepdims=True)
    exponent = jnp.exp(scores - row_max)
    row_sum = jnp.sum(exponent, axis=-1, keepdims=True)
    log_total = row_max + jnp.log(row_sum)
    attn_pb = (exponent / row_sum).astype(jnp.bfloat16)
    attn_o = jnp.einsum("hts,shd->thd", attn_pb, value_wide, preferred_element_type=jnp.float32)
    attn_ob = attn_o.reshape(tok_rows, model_width).astype(jnp.bfloat16)
    residual = inputs + jnp.dot(attn_ob, full_out, preferred_element_type=jnp.float32)
    h_two, norm_two_back = jax.vjp(layer_norm, residual, gain_pair[1])
    a_two = h_two.astype(jnp.bfloat16)
    gate = jnp.dot(a_two, full_gate, preferred_element_type=jnp.float32)
    linear = jnp.dot(a_two, full_lin, preferred_element_type=jnp.float32)
    middle, gelu_back = jax.vjp(gated_gelu, gate, linear)
    middle_b = middle.astype(jnp.bfloat16)
    outputs = (
        residual + jnp.einsum("tf,df->td", middle_b, full_mlp, preferred_element_type=jnp.float32)
    ).astype(
        jnp.bfloat16
    )
    back_qkv, back_out = (full_qkv, full_out)
    grad_out = cotangent[0].astype(jnp.float32)
    grad_mlp_b = grad_out.astype(jnp.bfloat16)
    grad_mid = jnp.dot(grad_mlp_b, full_mlp, preferred_element_type=jnp.float32)
    grad_gate_b, grad_lin_b = [g.astype(jnp.bfloat16) for g in gelu_back(grad_mid)]
    grad_a_two = jnp.einsum(
        "tf,df->td", grad_gate_b, full_gate, preferred_element_type=jnp.float32
    ) + jnp.einsum("tf,df->td", grad_lin_b, full_lin, preferred_element_type=jnp.float32)
    grad_res_norm, grad_gain_two = norm_two_back(grad_a_two)
    grad_res = grad_out + grad_res_norm
    grad_att_b = grad_res.astype(jnp.bfloat16)
    grad_o_b = jnp.einsum(
        "te,de->td", grad_att_b, back_out, preferred_element_type=jnp.float32
    ).astype(jnp.bfloat16)
    grad_o_heads = grad_o_b.reshape(tok_rows, HEADS, HD)
    scores_again = (
        jnp.einsum("thd,shd->hts", q_heads, key_wide, preferred_element_type=jnp.float32)
        * score_scale
    )
    scores_again = jnp.where(allowed[None], scores_again, masked_score)
    prob_again = jnp.exp(scores_again - log_total)
    grad_prob = jnp.einsum(
        "thd,shd->hts", grad_o_heads, value_wide, preferred_element_type=jnp.float32
    )
    delta_sum = jnp.sum(grad_prob * prob_again, axis=-1, keepdims=True)
    grad_scores_b = (prob_again * (grad_prob - delta_sum)).astype(jnp.bfloat16)
    grad_query = (
        jnp.einsum("hts,shd->thd", grad_scores_b, key_wide, preferred_element_type=jnp.float32)
        * score_scale
    )
    grad_key_wide = (
        jnp.einsum("hts,thd->shd", grad_scores_b, q_heads, preferred_element_type=jnp.float32)
        * score_scale
    )
    grad_value_wide = jnp.einsum(
        "hts,thd->shd", attn_pb, grad_o_heads, preferred_element_type=jnp.float32
    )
    grad_kv_wide = jnp.concatenate(
        [grad_key_wide.reshape(-1, model_width), grad_value_wide.reshape(-1, model_width)], axis=1
    )
    rim_grads = jnp.concatenate(
        [grad_kv_wide[:half_win], grad_kv_wide[tok_rows + half_win :]], axis=0
    )
    arrived = padded(rim_grads.astype(jnp.bfloat16), (("seq", 0),), half_win).astype(
        rim_grads.dtype
    )
    own_grads = grad_kv_wide[half_win : half_win + tok_rows]
    own_grads = own_grads + jnp.pad(arrived[:half_win], ((0, tok_rows - half_win), (0, 0)))
    own_grads = own_grads + jnp.pad(arrived[3 * half_win :], ((tok_rows - half_win, 0), (0, 0)))
    grad_qkv_b = jnp.concatenate(
        [
            rotate(grad_query.reshape(tok_rows, model_width), cos_table, -sin_table, HEADS),
            rotate(own_grads[:, :model_width], cos_table, -sin_table, HEADS),
            own_grads[:, model_width:],
        ],
        axis=1,
    ).astype(jnp.bfloat16)
    grad_a_one = jnp.einsum("te,de->td", grad_qkv_b, back_qkv, preferred_element_type=jnp.float32)
    grad_in_norm, grad_gain_one = norm_one_back(grad_a_one)
    input_grad = grad_res + grad_in_norm
    gains_cols = jnp.stack([grad_gain_one, grad_gain_two], axis=1)
    shares = lax.axis_size("fsdp") * lax.axis_size("seq")
    lefts = [a_one, attn_ob, a_two, grad_mlp_b]
    widths = [3 * model_width, model_width, 2 * ff_wide, ff_wide]
    rights = [
        grad_qkv_b,
        grad_att_b,
        jnp.concatenate([grad_gate_b, grad_lin_b], axis=1),
        middle_b,
    ]
    total_width = sum(widths) + tail
    fits = (
        lax.axis_size("seq") == 8
        and model_width % (16 * shares) == 0
        and total_width % (2 * LANE) == 0
        and all(w % SUB == 0 for w in widths[:3])
    )
    if fits:
        edges = [sum(widths[: i + 1]) // SUB for i in range(3)]
        summed = scatter_sums(
            jnp.stack([left.T for left in lefts]),
            jnp.concatenate(rights + [jnp.zeros((tok_rows, tail), jnp.bfloat16)], axis=1),
            jnp.pad(gains_cols, ((0, 0), (0, 128 - gains_cols.shape[1]))).astype(jnp.bfloat16),
            edges,
        )
        gains_at = total_width - 128
    else:
        summed = lax.psum_scatter(
            jnp.concatenate(
                [
                    jnp.einsum("td,te->de", left, right, preferred_element_type=jnp.float32)
                    for left, right in zip(lefts, rights)
                ]
                + [gains_cols],
                axis=1,
            ),
            ("fsdp", "seq"),
            scatter_dimension=0,
            tiled=True,
        )
        gains_at = sum(widths)
    edge_one = widths[0]
    edge_two = edge_one + widths[1]
    edge_three = edge_two + widths[2]
    sum_qkv = summed[:, :edge_one]
    sum_out = summed[:, edge_one:edge_two]
    sum_in = jnp.stack(
        [summed[:, edge_two : edge_two + ff], summed[:, edge_two + ff_wide : edge_two + ff_wide + ff]],
        axis=1,
    )
    sum_mlp = summed[:, edge_three : edge_three + ff].T
    sum_gains = summed[:, gains_at : gains_at + 2].T
    return (outputs[None], input_grad[None], sum_qkv, sum_out, sum_in, sum_mlp, sum_gains)


def solution(mesh):
    return jax.shard_map(
        local,
        mesh=mesh,
        in_specs=(
            P("fsdp", "seq", None),
            P("fsdp", None),
            P("fsdp", None),
            P("fsdp", None),
            P("fsdp", None, None),
            P(None, "fsdp"),
            P(None, "fsdp"),
            P("fsdp", "seq", None),
        ),
        out_specs=(
            P("fsdp", "seq", None),
            P("fsdp", "seq", None),
            P(("fsdp", "seq"), None),
            P(("fsdp", "seq"), None),
            P(("fsdp", "seq"), None, None),
            P(None, ("fsdp", "seq")),
            P(None, ("fsdp", "seq")),
        ),
        check_vma=False,
    )
```

```python
import functools

import jax
import jax.numpy as jnp
from jax import lax
from jax.experimental import pallas as pl
from jax.experimental.pallas import tpu as pltpu
from jax.sharding import PartitionSpec as P

HEADS = 16
HD = 64
WIN = 128


norm_eps = 1e-05
rope_base = 10000.0
masked_score = -1e30
MESH = pl.DeviceIdType.MESH
LANE = 1024
SUB = 256
LAGS = (6, 12)


def up_to(size, unit):
    return -(-size // unit) * unit


def gather_kernel(n, count, *refs):
    ins, outs = refs[:count], refs[count : 2 * count]
    z_send, z_recv, one_send, one_recv, two_send, two_recv, core_send, core_recv, own_sem = refs[
        2 * count : 2 * count + 9
    ]
    held = refs[2 * count + 9 :]
    me = lax.axis_index("fsdp")
    spot = lax.axis_index("seq")
    core = lax.rem(spot, 2)
    bit_x = lax.rem(spot // 2, 2)
    bit_y = lax.rem(spot // 4, 2)
    part = bit_y * 4 + bit_x * 2 + core
    base = spot - part
    height = ins[0].shape[0]
    block = height // 8

    def flip(number, mask):
        c = number % 2
        x = (number // 2) % 2
        y = number // 4
        c = 1 - c if mask & 1 else c
        x = 1 - x if mask & 2 else x
        y = 1 - y if mask & 4 else y
        return y * 4 + x * 2 + c

    mates = {mask: base + flip(part, mask) for mask in (1, 2, 4)}

    barrier = pltpu.get_barrier_semaphore()

    def greet(target):
        pl.semaphore_signal(barrier, inc=1, device_id=target, device_id_type=MESH)

    for mask in (1, 2, 4):
        greet((me, mates[mask]))

    @pl.when(me > 0)
    def _():
        greet((me - 1, spot))

    @pl.when(me < n - 1)
    def _():
        greet((me + 1, spot))

    peers = 3 + jnp.where(me > 0, 1, 0) + jnp.where(me < n - 1, 1, 0)
    pl.semaphore_wait(barrier, peers)

    def region(k, origin, mask):
        start = pl.multiple_of(origin * height + flip(part, mask) * block, block)
        return outs[k].at[pl.ds(start, block)]

    def remote(src, dst, send, recv, target):
        return pltpu.make_async_remote_copy(
            src_ref=src, dst_ref=dst, send_sem=send, recv_sem=recv, device_id=target, device_id_type=MESH
        )

    def z_copy(way, origin, k, own=False):
        if own:
            src = ins[k].at[pl.ds(pl.multiple_of(part * block, block), block)]
        else:
            src = region(k, origin, 0)
        target = me + 1 if way == 0 else me - 1
        return remote(
            src, region(k, origin, 0), z_send.at[way, origin, k], z_recv.at[origin, k], (target, spot)
        )

    def firsts(k):
        return (2, 4) if k % 2 == 0 else (4, 2)

    def one_copy(origin, k, mask=0):
        place = region(k, origin, mask)
        return remote(
            place, place, one_send.at[origin, k], one_recv.at[origin, k], (me, mates[firsts(k)[0]])
        )

    def two_copy(origin, k, index, mask):
        place = region(k, origin, mask)
        return remote(
            place,
            place,
            two_send.at[origin, k, index],
            two_recv.at[origin, k, index],
            (me, mates[firsts(k)[1]]),
        )

    def core_copy(origin, k, index, mask):
        place = region(k, origin, mask)
        return remote(
            place,
            place,
            core_send.at[origin, k, index],
            core_recv.at[origin, k, index],
            (me, mates[1]),
        )

    def can_go(way):
        return me < n - 1 if way == 0 else me > 0

    def has(way, d):
        return me >= d if way == 0 else me + d <= n - 1

    for k in range(count):
        for way in (0, 1):

            @pl.when(can_go(way))
            def _(k=k, way=way):
                z_copy(way, me, k, own=True).start()

    def own_in(k):
        return pltpu.make_async_copy(ins[k], held[k], own_sem.at[0, k])

    def own_out(k):
        rows = pl.ds(pl.multiple_of(me * height, height), height)
        return pltpu.make_async_copy(held[k], outs[k].at[rows], own_sem.at[1, k])

    for k in range(count):
        own_in(k).start()
    for k in range(count):
        own_in(k).wait()
        own_out(k).start()

    def came(way, d, k):
        origin = me - d if way == 0 else me + d

        @pl.when(has(way, d))
        def _():
            z_copy(way, origin, k).wait_recv()

            @pl.when(can_go(way))
            def _():
                z_copy(way, origin, k).start()

            one_copy(origin, k).start()
            two_copy(origin, k, 0, 0).start()
            core_copy(origin, k, 0, 0).start()

    def second(way, d, k):
        origin = me - d if way == 0 else me + d
        m_one, m_two = firsts(k)

        @pl.when(has(way, d))
        def _():
            one_copy(origin, k, m_one).wait_recv()
            two_copy(origin, k, 1, m_one).start()
            core_copy(origin, k, 1, m_one).start()

    def third(way, d, k):
        origin = me - d if way == 0 else me + d
        m_one, m_two = firsts(k)

        @pl.when(has(way, d))
        def _():
            two_copy(origin, k, 0, m_two).wait_recv()
            core_copy(origin, k, 2, m_two).start()
            two_copy(origin, k, 1, m_one + m_two).wait_recv()
            core_copy(origin, k, 3, m_one + m_two).start()

    def last(way, d, k):
        origin = me - d if way == 0 else me + d
        m_one, m_two = firsts(k)
        masks = (0, m_one, m_two, m_one + m_two)

        @pl.when(has(way, d))
        def _():
            for index, mask in enumerate(masks):
                core_copy(origin, k, index, mask + 1).wait_recv()
                core_copy(origin, k, index, mask).wait_send()
            one_copy(origin, k).wait_send()
            two_copy(origin, k, 0, 0).wait_send()
            two_copy(origin, k, 1, m_one).wait_send()

            @pl.when(can_go(way))
            def _():
                z_copy(way, origin, k).wait_send()

    steps = [(way, d, k) for d in range(1, n) for k in range(count) for way in (0, 1)]
    lag_one, lag_two = LAGS
    total = len(steps)
    for i in range(total + lag_two):
        if i < total:
            came(*steps[i])
        if 0 <= i - lag_one < total:
            second(*steps[i - lag_one])
        if 0 <= i - lag_two < total:
            third(*steps[i - lag_two])
    for step in steps:
        last(*step)
    for k in range(count):
        for way in (0, 1):

            @pl.when(can_go(way))
            def _(k=k, way=way):
                z_copy(way, me, k, own=True).wait_send()

        own_out(k).wait()


def gather_weights(shards):
    n = lax.axis_size("fsdp")
    count = len(shards)
    sem = pltpu.SemaphoreType.DMA
    return pl.pallas_call(
        functools.partial(gather_kernel, n, count),
        out_shape=[jax.ShapeDtypeStruct((n * s.shape[0], s.shape[1]), s.dtype) for s in shards],
        in_specs=[pl.BlockSpec(memory_space=pl.ANY)] * count,
        out_specs=[pl.BlockSpec(memory_space=pl.ANY)] * count,
        scratch_shapes=[
            sem((2, n, count)),
            sem((n, count)),
            sem((n, count)),
            sem((n, count)),
            sem((n, count, 2)),
            sem((n, count, 2)),
            sem((n, count, 4)),
            sem((n, count, 4)),
            sem((2, count)),
        ]
        + [pltpu.VMEM(s.shape, s.dtype) for s in shards],
        compiler_params=pltpu.CompilerParams(
            collective_id=0, has_side_effects=True, vmem_limit_bytes=32 * 1024 * 1024
        ),
        name="gather_weights",
    )(*shards)


def scatter_kernel(
    n, edges, at_ref, b_ref, gcol_ref, out_ref,
    gbuf, r_core, r_one, r_two, r_z,
    core_send, core_recv, one_send, one_recv, two_send, two_recv, z_send, z_recv,
):
    me = lax.axis_index("fsdp")
    spot = lax.axis_index("seq")
    c = lax.rem(spot, 2)
    x = lax.rem(spot // 2, 2)
    y = spot // 4
    r = gbuf.shape[5]
    chunks = gbuf.shape[0]
    units = chunks // 2
    mate_c = y * 4 + x * 2 + (1 - c)
    mate_x = y * 4 + (1 - x) * 2 + c
    mate_y = (1 - y) * 4 + x * 2 + c

    barrier = pltpu.get_barrier_semaphore()
    for mate in (mate_c, mate_x, mate_y):
        pl.semaphore_signal(barrier, inc=1, device_id=(me, mate), device_id_type=MESH)
    for d in range(1, n):
        pl.semaphore_signal(
            barrier, inc=1, device_id=(lax.rem(me + d, n), spot), device_id_type=MESH
        )
    pl.semaphore_wait(barrier, 3 + n - 1)

    def remote(src, dst, send, recv, target):
        return pltpu.make_async_remote_copy(
            src_ref=src, dst_ref=dst, send_sem=send, recv_sem=recv, device_id=target, device_id_type=MESH
        )

    def core_copy(j):
        return remote(
            gbuf.at[j, :, :, :, 1 - c], r_core.at[j], core_send.at[j], core_recv.at[j], (me, mate_c)
        )

    def one_copy(j, e):
        src = gbuf.at[j, :, :, 1 - x, c] if e == 0 else gbuf.at[j, :, 1 - y, :, c]
        mate = mate_x if e == 0 else mate_y
        return remote(src, r_one.at[j], one_send.at[j], one_recv.at[j], (me, mate))

    def two_copy(j, e):
        src = gbuf.at[j, :, 1 - y, x, c] if e == 0 else gbuf.at[j, :, y, 1 - x, c]
        mate = mate_y if e == 0 else mate_x
        return remote(src, r_two.at[j], two_send.at[j], two_recv.at[j], (me, mate))

    def z_copy(j, d):
        other = lax.rem(me + d, n)
        return remote(
            gbuf.at[j, other, y, x, c],
            r_z.at[j, d - 1],
            z_send.at[j, d - 1],
            z_recv.at[j, d - 1],
            (other, spot),
        )

    def plus(left, right):
        return (left.astype(jnp.float32) + right.astype(jnp.float32)).astype(left.dtype)

    def make(k):
        def one_tile(u, carry):
            t = k * (2 * LANE // SUB) + u
            which = jnp.int32(0)
            for edge in edges:
                which = which + jnp.where(t >= edge, 1, 0).astype(jnp.int32)
            columns = pl.ds(pl.multiple_of(t * SUB, SUB), SUB)
            value = jnp.dot(at_ref[which], b_ref[:, columns], preferred_element_type=jnp.float32)
            value = value.astype(gbuf.dtype).reshape(gbuf.shape[1:6] + (SUB,))
            j = k * 2 + u // (LANE // SUB)
            inner = pl.ds(pl.multiple_of((u % (LANE // SUB)) * SUB, SUB), SUB)
            gbuf[j, :, :, :, :, :, inner] = value
            return carry

        lax.fori_loop(0, 2 * LANE // SUB, one_tile, 0)

    def turn(it, carry):
        @pl.when(it < units)
        def _():
            make(it)

            @pl.when(it == units - 1)
            def _():
                wide = gcol_ref.shape[1]
                gbuf[chunks - 1, :, :, :, :, :, LANE - wide :] = gcol_ref[...].reshape(
                    gbuf.shape[1:6] + (wide,)
                )

            core_copy(2 * it).start()
            core_copy(2 * it + 1).start()

        @pl.when((it >= 1) & (it < units + 1))
        def _():
            for e in (0, 1):
                j = 2 * (it - 1) + e
                core_copy(j).wait()
                for i in range(n):
                    for a in (0, 1):
                        gbuf[j, i, a, :, c] = plus(gbuf[j, i, a, :, c], r_core[j, i, a])
                one_copy(j, e).start()

        @pl.when((it >= 2) & (it < units + 2))
        def _():
            for e in (0, 1):
                j = 2 * (it - 2) + e
                one_copy(j, e).wait()
                for i in range(n):
                    if e == 0:
                        gbuf[j, i, :, x, c] = plus(gbuf[j, i, :, x, c], r_one[j, i])
                    else:
                        gbuf[j, i, y, :, c] = plus(gbuf[j, i, y, :, c], r_one[j, i])
                two_copy(j, e).start()

        @pl.when((it >= 3) & (it < units + 3))
        def _():
            for e in (0, 1):
                j = 2 * (it - 3) + e
                two_copy(j, e).wait()
                for i in range(n):
                    gbuf[j, i, y, x, c] = plus(gbuf[j, i, y, x, c], r_two[j, i])
                for d in range(1, n):
                    z_copy(j, d).start()

        @pl.when(it >= 4)
        def _():
            for e in (0, 1):
                j = 2 * (it - 4) + e
                total = gbuf[j, me, y, x, c].astype(jnp.float32)
                for d in range(1, n):
                    z_copy(j, d).wait()
                    total = total + r_z[j, d - 1].astype(jnp.float32)
                out_ref[:, pl.ds(pl.multiple_of(j * LANE, LANE), LANE)] = total

        return carry

    lax.fori_loop(0, units + 4, turn, 0)


def scatter_sums(lefts, rights, gain_columns, edges):
    n = lax.axis_size("fsdp")
    rows = lefts.shape[1]
    r = rows // (8 * n)
    width = rights.shape[1]
    chunks = width // LANE
    half = jnp.bfloat16
    sem = pltpu.SemaphoreType.DMA
    vmem = pl.BlockSpec(memory_space=pltpu.VMEM)
    return pl.pallas_call(
        functools.partial(scatter_kernel, n, edges),
        out_shape=jax.ShapeDtypeStruct((r, width), jnp.float32),
        in_specs=[vmem] * 3,
        out_specs=vmem,
        scratch_shapes=[
            pltpu.VMEM((chunks, n, 2, 2, 2, r, LANE), half),
            pltpu.VMEM((chunks, n, 2, 2, r, LANE), half),
            pltpu.VMEM((chunks, n, 2, r, LANE), half),
            pltpu.VMEM((chunks, n, r, LANE), half),
            pltpu.VMEM((chunks, n - 1, r, LANE), half),
            sem((chunks,)),
            sem((chunks,)),
            sem((chunks,)),
            sem((chunks,)),
            sem((chunks,)),
            sem((chunks,)),
            sem((chunks, n - 1)),
            sem((chunks, n - 1)),
        ],
        compiler_params=pltpu.CompilerParams(
            collective_id=1, has_side_effects=True, vmem_limit_bytes=62 * 1024 * 1024
        ),
        name="scatter_sums",
    )(lefts, rights, gain_columns)


def padded(cells, sides, width):
    for axis, dim in sides:
        count = lax.axis_size(axis)
        ends = count - 1
        head = lax.slice_in_dim(cells, 0, width, axis=dim)
        tail = lax.slice_in_dim(cells, cells.shape[dim] - width, cells.shape[dim], axis=dim)
        cells = jnp.concatenate(
            [
                lax.ppermute(tail, axis, [(i, (i + 1) % count) for i in range(ends)]),
                cells,
                lax.ppermute(head, axis, [((i + 1) % count, i) for i in range(ends)]),
            ],
            axis=dim,
        )
    return cells


def layer_norm(values, norm_gain):
    centre = values - jnp.mean(values, axis=-1, keepdims=True)
    spread = jnp.mean(centre * centre, axis=-1, keepdims=True)
    return centre * lax.rsqrt(spread + norm_eps) * norm_gain


def rope_tables(positions, head_dim):
    half_dim = head_dim // 2
    inv_freq = rope_base ** (-(2.0 * jnp.arange(half_dim, dtype=jnp.float32)) / head_dim)
    angles = positions.astype(jnp.float32)[:, None] * inv_freq[None, :]
    return (jnp.cos(angles), jnp.sin(angles))


def rotate(values, cos_table, sin_table, head_count):
    tok_rows = values.shape[0]
    shaped = values.reshape(tok_rows, head_count, -1)
    half_dim = shaped.shape[-1] // 2
    first_half = shaped[..., :half_dim]
    second = shaped[..., half_dim:]
    cos_part = cos_table[:, None, :]
    sin_part = sin_table[:, None, :]
    turned = jnp.concatenate(
        [first_half * cos_part - second * sin_part, second * cos_part + first_half * sin_part],
        axis=-1,
    )
    return turned.reshape(tok_rows, -1)


def gated_gelu(gate, linear):
    return jax.nn.gelu(gate, approximate=False) * linear


def local(tokens, segment_ids, w_qkv, w_attn_out, w_in, w_mlp_out, norm_gains, cotangent):
    tok_rows = tokens.shape[1]
    model_width = tokens.shape[2]
    half_win = WIN // 2
    score_scale = HD ** (-0.5)
    row_start = lax.axis_index("seq") * tok_rows
    ff = w_in.shape[2]
    ff_wide = up_to(ff, 128)
    tail = up_to(ff_wide + 128, SUB) - ff_wide
    stretch = ((0, 0), (0, ff_wide - ff))
    full_qkv, full_out, full_gate, full_lin, full_down = gather_weights(
        [
            w_qkv,
            w_attn_out,
            jnp.pad(w_in[:, 0], stretch),
            jnp.pad(w_in[:, 1], stretch),
            jnp.concatenate(
                [
                    jnp.pad(w_mlp_out.T, stretch),
                    jnp.pad(norm_gains.T, ((0, 0), (0, tail - norm_gains.shape[0]))),
                ],
                axis=1,
            ),
        ]
    )
    full_mlp = full_down[:, :ff_wide]
    gain_pair = full_down[:, ff_wide : ff_wide + norm_gains.shape[0]].T.astype(jnp.float32)
    inputs = tokens[0].astype(jnp.float32)
    cos_table, sin_table = rope_tables(row_start + jnp.arange(tok_rows, dtype=jnp.int32), HD)
    h_one, norm_one_back = jax.vjp(layer_norm, inputs, gain_pair[0])
    a_one = h_one.astype(jnp.bfloat16)
    qkv_full = jnp.dot(a_one, full_qkv, preferred_element_type=jnp.float32)
    query_rows = rotate(qkv_full[:, :model_width], cos_table, sin_table, HEADS).astype(jnp.bfloat16)
    key_rows = rotate(
        qkv_full[:, model_width : 2 * model_width], cos_table, sin_table, HEADS
    ).astype(jnp.bfloat16)
    value_rows = qkv_full[:, 2 * model_width :].astype(jnp.bfloat16)
    kv_wide = padded(jnp.concatenate([key_rows, value_rows], axis=1), (("seq", 0),), half_win)
    key_wide = kv_wide[:, :model_width].reshape(-1, HEADS, HD)
    value_wide = kv_wide[:, model_width:].reshape(-1, HEADS, HD)
    row_ids = segment_ids[0]
    ids_pad = jnp.pad(row_ids, (half_win, half_win), constant_values=-1)
    k_ids = lax.dynamic_slice_in_dim(ids_pad, row_start, tok_rows + 2 * half_win)
    q_ids = lax.dynamic_slice_in_dim(row_ids, row_start, tok_rows)
    offsets = (
        jnp.arange(tok_rows)[:, None] - jnp.arange(tok_rows + 2 * half_win)[None, :] + half_win
    )
    allowed = (jnp.abs(offsets) <= half_win) & (q_ids[:, None] == k_ids[None, :])
    q_heads = query_rows.reshape(tok_rows, HEADS, HD)
    scores = (
        jnp.einsum("thd,shd->hts", q_heads, key_wide, preferred_element_type=jnp.float32)
        * score_scale
    )
    scores = jnp.where(allowed[None], scores, masked_score)
    row_max = jnp.max(scores, axis=-1, keepdims=True)
    exponent = jnp.exp(scores - row_max)
    row_sum = jnp.sum(exponent, axis=-1, keepdims=True)
    log_total = row_max + jnp.log(row_sum)
    attn_pb = (exponent / row_sum).astype(jnp.bfloat16)
    attn_o = jnp.einsum("hts,shd->thd", attn_pb, value_wide, preferred_element_type=jnp.float32)
    attn_ob = attn_o.reshape(tok_rows, model_width).astype(jnp.bfloat16)
    residual = inputs + jnp.dot(attn_ob, full_out, preferred_element_type=jnp.float32)
    h_two, norm_two_back = jax.vjp(layer_norm, residual, gain_pair[1])
    a_two = h_two.astype(jnp.bfloat16)
    gate = jnp.dot(a_two, full_gate, preferred_element_type=jnp.float32)
    linear = jnp.dot(a_two, full_lin, preferred_element_type=jnp.float32)
    middle, gelu_back = jax.vjp(gated_gelu, gate, linear)
    middle_b = middle.astype(jnp.bfloat16)
    outputs = (
        residual + jnp.einsum("tf,df->td", middle_b, full_mlp, preferred_element_type=jnp.float32)
    ).astype(
        jnp.bfloat16
    )
    back_qkv, back_out = (full_qkv, full_out)
    grad_out = cotangent[0].astype(jnp.float32)
    grad_mlp_b = grad_out.astype(jnp.bfloat16)
    grad_mid = jnp.dot(grad_mlp_b, full_mlp, preferred_element_type=jnp.float32)
    grad_gate_b, grad_lin_b = [g.astype(jnp.bfloat16) for g in gelu_back(grad_mid)]
    grad_a_two = jnp.einsum(
        "tf,df->td", grad_gate_b, full_gate, preferred_element_type=jnp.float32
    ) + jnp.einsum("tf,df->td", grad_lin_b, full_lin, preferred_element_type=jnp.float32)
    grad_res_norm, grad_gain_two = norm_two_back(grad_a_two)
    grad_res = grad_out + grad_res_norm
    grad_att_b = grad_res.astype(jnp.bfloat16)
    grad_o_b = jnp.einsum(
        "te,de->td", grad_att_b, back_out, preferred_element_type=jnp.float32
    ).astype(jnp.bfloat16)
    grad_o_heads = grad_o_b.reshape(tok_rows, HEADS, HD)
    scores_again = (
        jnp.einsum("thd,shd->hts", q_heads, key_wide, preferred_element_type=jnp.float32)
        * score_scale
    )
    scores_again = jnp.where(allowed[None], scores_again, masked_score)
    prob_again = jnp.exp(scores_again - log_total)
    grad_prob = jnp.einsum(
        "thd,shd->hts", grad_o_heads, value_wide, preferred_element_type=jnp.float32
    )
    delta_sum = jnp.sum(grad_prob * prob_again, axis=-1, keepdims=True)
    grad_scores_b = (prob_again * (grad_prob - delta_sum)).astype(jnp.bfloat16)
    grad_query = (
        jnp.einsum("hts,shd->thd", grad_scores_b, key_wide, preferred_element_type=jnp.float32)
        * score_scale
    )
    grad_key_wide = (
        jnp.einsum("hts,thd->shd", grad_scores_b, q_heads, preferred_element_type=jnp.float32)
        * score_scale
    )
    grad_value_wide = jnp.einsum(
        "hts,thd->shd", attn_pb, grad_o_heads, preferred_element_type=jnp.float32
    )
    grad_kv_wide = jnp.concatenate(
        [grad_key_wide.reshape(-1, model_width), grad_value_wide.reshape(-1, model_width)], axis=1
    )
    rim_grads = jnp.concatenate(
        [grad_kv_wide[:half_win], grad_kv_wide[tok_rows + half_win :]], axis=0
    )
    arrived = padded(rim_grads.astype(jnp.bfloat16), (("seq", 0),), half_win).astype(
        rim_grads.dtype
    )
    own_grads = grad_kv_wide[half_win : half_win + tok_rows]
    own_grads = own_grads + jnp.pad(arrived[:half_win], ((0, tok_rows - half_win), (0, 0)))
    own_grads = own_grads + jnp.pad(arrived[3 * half_win :], ((tok_rows - half_win, 0), (0, 0)))
    grad_qkv_b = jnp.concatenate(
        [
            rotate(grad_query.reshape(tok_rows, model_width), cos_table, -sin_table, HEADS),
            rotate(own_grads[:, :model_width], cos_table, -sin_table, HEADS),
            own_grads[:, model_width:],
        ],
        axis=1,
    ).astype(jnp.bfloat16)
    grad_a_one = jnp.einsum("te,de->td", grad_qkv_b, back_qkv, preferred_element_type=jnp.float32)
    grad_in_norm, grad_gain_one = norm_one_back(grad_a_one)
    input_grad = grad_res + grad_in_norm
    gains_cols = jnp.stack([grad_gain_one, grad_gain_two], axis=1)
    shares = lax.axis_size("fsdp") * lax.axis_size("seq")
    lefts = [a_one, attn_ob, a_two, grad_mlp_b]
    widths = [3 * model_width, model_width, 2 * ff_wide, ff_wide]
    rights = [
        grad_qkv_b,
        grad_att_b,
        jnp.concatenate([grad_gate_b, grad_lin_b], axis=1),
        middle_b,
    ]
    total_width = sum(widths) + tail
    fits = (
        lax.axis_size("seq") == 8
        and model_width % (16 * shares) == 0
        and total_width % (2 * LANE) == 0
        and all(w % SUB == 0 for w in widths[:3])
    )
    if fits:
        edges = [sum(widths[: i + 1]) // SUB for i in range(3)]
        summed = scatter_sums(
            jnp.stack([left.T for left in lefts]),
            jnp.concatenate(rights + [jnp.zeros((tok_rows, tail), jnp.bfloat16)], axis=1),
            jnp.pad(gains_cols, ((0, 0), (0, 128 - gains_cols.shape[1]))).astype(jnp.bfloat16),
            edges,
        )
        gains_at = total_width - 128
    else:
        summed = lax.psum_scatter(
            jnp.concatenate(
                [
                    jnp.einsum("td,te->de", left, right, preferred_element_type=jnp.float32)
                    for left, right in zip(lefts, rights)
                ]
                + [gains_cols],
                axis=1,
            ),
            ("fsdp", "seq"),
            scatter_dimension=0,
            tiled=True,
        )
        gains_at = sum(widths)
    edge_one = widths[0]
    edge_two = edge_one + widths[1]
    edge_three = edge_two + widths[2]
    sum_qkv = summed[:, :edge_one]
    sum_out = summed[:, edge_one:edge_two]
    sum_in = jnp.stack(
        [summed[:, edge_two : edge_two + ff], summed[:, edge_two + ff_wide : edge_two + ff_wide + ff]],
        axis=1,
    )
    sum_mlp = summed[:, edge_three : edge_three + ff].T
    sum_gains = summed[:, gains_at : gains_at + 2].T
    return (outputs[None], input_grad[None], sum_qkv, sum_out, sum_in, sum_mlp, sum_gains)


def solution(mesh):
    return jax.shard_map(
        local,
        mesh=mesh,
        in_specs=(
            P("fsdp", "seq", None),
            P("fsdp", None),
            P("fsdp", None),
            P("fsdp", None),
            P("fsdp", None, None),
            P(None, "fsdp"),
            P(None, "fsdp"),
            P("fsdp", "seq", None),
        ),
        out_specs=(
            P("fsdp", "seq", None),
            P("fsdp", "seq", None),
            P(("fsdp", "seq"), None),
            P(("fsdp", "seq"), None),
            P(("fsdp", "seq"), None, None),
            P(None, ("fsdp", "seq")),
            P(None, ("fsdp", "seq")),
        ),
        check_vma=False,
    )
```

```python
import functools

import jax
import jax.numpy as jnp
from jax import lax
from jax.experimental import pallas as pl
from jax.experimental.pallas import tpu as pltpu
from jax.sharding import PartitionSpec as P

HEADS = 16
HD = 64
WIN = 128


norm_eps = 1e-05
rope_base = 10000.0
masked_score = -1e30
MESH = pl.DeviceIdType.MESH
LANE = 1024
SUB = 256
LAGS = (6, 12)


def up_to(size, unit):
    return -(-size // unit) * unit


def gather_kernel(n, count, *refs):
    ins, outs = refs[:count], refs[count : 2 * count]
    z_send, z_recv, one_send, one_recv, two_send, two_recv, core_send, core_recv, own_sem = refs[
        2 * count : 2 * count + 9
    ]
    held = refs[2 * count + 9 :]
    me = lax.axis_index("fsdp")
    spot = lax.axis_index("seq")
    core = lax.rem(spot, 2)
    bit_x = lax.rem(spot // 2, 2)
    bit_y = lax.rem(spot // 4, 2)
    part = bit_y * 4 + bit_x * 2 + core
    base = spot - part
    height = ins[0].shape[0]
    block = height // 8

    def flip(number, mask):
        c = number % 2
        x = (number // 2) % 2
        y = number // 4
        c = 1 - c if mask & 1 else c
        x = 1 - x if mask & 2 else x
        y = 1 - y if mask & 4 else y
        return y * 4 + x * 2 + c

    mates = {mask: base + flip(part, mask) for mask in (1, 2, 4)}

    barrier = pltpu.get_barrier_semaphore()

    def greet(target):
        pl.semaphore_signal(barrier, inc=1, device_id=target, device_id_type=MESH)

    for mask in (1, 2, 4):
        greet((me, mates[mask]))

    @pl.when(me > 0)
    def _():
        greet((me - 1, spot))

    @pl.when(me < n - 1)
    def _():
        greet((me + 1, spot))

    peers = 3 + jnp.where(me > 0, 1, 0) + jnp.where(me < n - 1, 1, 0)
    pl.semaphore_wait(barrier, peers)

    def region(k, origin, mask):
        start = pl.multiple_of(origin * height + flip(part, mask) * block, block)
        return outs[k].at[pl.ds(start, block)]

    def remote(src, dst, send, recv, target):
        return pltpu.make_async_remote_copy(
            src_ref=src, dst_ref=dst, send_sem=send, recv_sem=recv, device_id=target, device_id_type=MESH
        )

    def z_copy(way, origin, k, own=False):
        if own:
            src = ins[k].at[pl.ds(pl.multiple_of(part * block, block), block)]
        else:
            src = region(k, origin, 0)
        target = me + 1 if way == 0 else me - 1
        return remote(
            src, region(k, origin, 0), z_send.at[way, origin, k], z_recv.at[origin, k], (target, spot)
        )

    def firsts(k):
        return (2, 4) if k % 2 == 0 else (4, 2)

    def one_copy(origin, k, mask=0):
        place = region(k, origin, mask)
        return remote(
            place, place, one_send.at[origin, k], one_recv.at[origin, k], (me, mates[firsts(k)[0]])
        )

    def two_copy(origin, k, index, mask):
        place = region(k, origin, mask)
        return remote(
            place,
            place,
            two_send.at[origin, k, index],
            two_recv.at[origin, k, index],
            (me, mates[firsts(k)[1]]),
        )

    def core_copy(origin, k, index, mask):
        place = region(k, origin, mask)
        return remote(
            place,
            place,
            core_send.at[origin, k, index],
            core_recv.at[origin, k, index],
            (me, mates[1]),
        )

    def can_go(way):
        return me < n - 1 if way == 0 else me > 0

    def has(way, d):
        return me >= d if way == 0 else me + d <= n - 1

    for k in range(count):
        for way in (0, 1):

            @pl.when(can_go(way))
            def _(k=k, way=way):
                z_copy(way, me, k, own=True).start()

    def own_in(k):
        return pltpu.make_async_copy(ins[k], held[k], own_sem.at[0, k])

    def own_out(k):
        rows = pl.ds(pl.multiple_of(me * height, height), height)
        return pltpu.make_async_copy(held[k], outs[k].at[rows], own_sem.at[1, k])

    for k in range(count):
        own_in(k).start()
    for k in range(count):
        own_in(k).wait()
        own_out(k).start()

    def came(way, d, k):
        origin = me - d if way == 0 else me + d

        @pl.when(has(way, d))
        def _():
            z_copy(way, origin, k).wait_recv()

            @pl.when(can_go(way))
            def _():
                z_copy(way, origin, k).start()

            one_copy(origin, k).start()
            two_copy(origin, k, 0, 0).start()
            core_copy(origin, k, 0, 0).start()

    def second(way, d, k):
        origin = me - d if way == 0 else me + d
        m_one, m_two = firsts(k)

        @pl.when(has(way, d))
        def _():
            one_copy(origin, k, m_one).wait_recv()
            two_copy(origin, k, 1, m_one).start()
            core_copy(origin, k, 1, m_one).start()

    def third(way, d, k):
        origin = me - d if way == 0 else me + d
        m_one, m_two = firsts(k)

        @pl.when(has(way, d))
        def _():
            two_copy(origin, k, 0, m_two).wait_recv()
            core_copy(origin, k, 2, m_two).start()
            two_copy(origin, k, 1, m_one + m_two).wait_recv()
            core_copy(origin, k, 3, m_one + m_two).start()

    def last(way, d, k):
        origin = me - d if way == 0 else me + d
        m_one, m_two = firsts(k)
        masks = (0, m_one, m_two, m_one + m_two)

        @pl.when(has(way, d))
        def _():
            for index, mask in enumerate(masks):
                core_copy(origin, k, index, mask + 1).wait_recv()
                core_copy(origin, k, index, mask).wait_send()
            one_copy(origin, k).wait_send()
            two_copy(origin, k, 0, 0).wait_send()
            two_copy(origin, k, 1, m_one).wait_send()

            @pl.when(can_go(way))
            def _():
                z_copy(way, origin, k).wait_send()

    steps = [(way, d, k) for d in range(1, n) for k in range(count) for way in (0, 1)]
    lag_one, lag_two = LAGS
    total = len(steps)
    for i in range(total + lag_two):
        if i < total:
            came(*steps[i])
        if 0 <= i - lag_one < total:
            second(*steps[i - lag_one])
        if 0 <= i - lag_two < total:
            third(*steps[i - lag_two])
    for step in steps:
        last(*step)
    for k in range(count):
        for way in (0, 1):

            @pl.when(can_go(way))
            def _(k=k, way=way):
                z_copy(way, me, k, own=True).wait_send()

        own_out(k).wait()


def gather_weights(shards):
    n = lax.axis_size("fsdp")
    count = len(shards)
    sem = pltpu.SemaphoreType.DMA
    return pl.pallas_call(
        functools.partial(gather_kernel, n, count),
        out_shape=[jax.ShapeDtypeStruct((n * s.shape[0], s.shape[1]), s.dtype) for s in shards],
        in_specs=[pl.BlockSpec(memory_space=pl.ANY)] * count,
        out_specs=[pl.BlockSpec(memory_space=pl.ANY)] * count,
        scratch_shapes=[
            sem((2, n, count)),
            sem((n, count)),
            sem((n, count)),
            sem((n, count)),
            sem((n, count, 2)),
            sem((n, count, 2)),
            sem((n, count, 4)),
            sem((n, count, 4)),
            sem((2, count)),
        ]
        + [pltpu.VMEM(s.shape, s.dtype) for s in shards],
        compiler_params=pltpu.CompilerParams(
            collective_id=0, has_side_effects=True, vmem_limit_bytes=32 * 1024 * 1024
        ),
        name="gather_weights",
    )(*shards)


def scatter_kernel(
    n, edges, at_ref, b_ref, gcol_ref, out_ref,
    gbuf, r_core, r_one, r_two, r_z,
    core_send, core_recv, one_send, one_recv, two_send, two_recv, z_send, z_recv,
):
    me = lax.axis_index("fsdp")
    spot = lax.axis_index("seq")
    c = lax.rem(spot, 2)
    x = lax.rem(spot // 2, 2)
    y = spot // 4
    r = gbuf.shape[5]
    chunks = gbuf.shape[0]
    units = chunks // 2
    mate_c = y * 4 + x * 2 + (1 - c)
    mate_x = y * 4 + (1 - x) * 2 + c
    mate_y = (1 - y) * 4 + x * 2 + c

    barrier = pltpu.get_barrier_semaphore()
    for mate in (mate_c, mate_x, mate_y):
        pl.semaphore_signal(barrier, inc=1, device_id=(me, mate), device_id_type=MESH)
    for d in range(1, n):
        pl.semaphore_signal(
            barrier, inc=1, device_id=(lax.rem(me + d, n), spot), device_id_type=MESH
        )
    pl.semaphore_wait(barrier, 3 + n - 1)

    def remote(src, dst, send, recv, target):
        return pltpu.make_async_remote_copy(
            src_ref=src, dst_ref=dst, send_sem=send, recv_sem=recv, device_id=target, device_id_type=MESH
        )

    def core_copy(j):
        return remote(
            gbuf.at[j, :, :, :, 1 - c], r_core.at[j], core_send.at[j], core_recv.at[j], (me, mate_c)
        )

    def one_copy(j, e):
        src = gbuf.at[j, :, :, 1 - x, c] if e == 0 else gbuf.at[j, :, 1 - y, :, c]
        mate = mate_x if e == 0 else mate_y
        return remote(src, r_one.at[j], one_send.at[j], one_recv.at[j], (me, mate))

    def two_copy(j, e):
        src = gbuf.at[j, :, 1 - y, x, c] if e == 0 else gbuf.at[j, :, y, 1 - x, c]
        mate = mate_y if e == 0 else mate_x
        return remote(src, r_two.at[j], two_send.at[j], two_recv.at[j], (me, mate))

    def z_copy(j, d):
        other = lax.rem(me + d, n)
        return remote(
            gbuf.at[j, other, y, x, c],
            r_z.at[j, d - 1],
            z_send.at[j, d - 1],
            z_recv.at[j, d - 1],
            (other, spot),
        )

    def plus(left, right):
        return (left.astype(jnp.float32) + right.astype(jnp.float32)).astype(left.dtype)

    def make(k):
        def one_tile(u, carry):
            t = k * (2 * LANE // SUB) + u
            which = jnp.int32(0)
            for edge in edges:
                which = which + jnp.where(t >= edge, 1, 0).astype(jnp.int32)
            columns = pl.ds(pl.multiple_of(t * SUB, SUB), SUB)
            value = jnp.dot(at_ref[which], b_ref[:, columns], preferred_element_type=jnp.float32)
            value = value.astype(gbuf.dtype).reshape(gbuf.shape[1:6] + (SUB,))
            j = k * 2 + u // (LANE // SUB)
            inner = pl.ds(pl.multiple_of((u % (LANE // SUB)) * SUB, SUB), SUB)
            gbuf[j, :, :, :, :, :, inner] = value
            return carry

        lax.fori_loop(0, 2 * LANE // SUB, one_tile, 0)

    def turn(it, carry):
        @pl.when(it < units)
        def _():
            make(it)

            @pl.when(it == units - 1)
            def _():
                wide = gcol_ref.shape[1]
                gbuf[chunks - 1, :, :, :, :, :, LANE - wide :] = gcol_ref[...].reshape(
                    gbuf.shape[1:6] + (wide,)
                )

            core_copy(2 * it).start()
            core_copy(2 * it + 1).start()

        @pl.when((it >= 1) & (it < units + 1))
        def _():
            for e in (0, 1):
                j = 2 * (it - 1) + e
                core_copy(j).wait()
                for i in range(n):
                    for a in (0, 1):
                        gbuf[j, i, a, :, c] = plus(gbuf[j, i, a, :, c], r_core[j, i, a])
                one_copy(j, e).start()

        @pl.when((it >= 2) & (it < units + 2))
        def _():
            for e in (0, 1):
                j = 2 * (it - 2) + e
                one_copy(j, e).wait()
                for i in range(n):
                    if e == 0:
                        gbuf[j, i, :, x, c] = plus(gbuf[j, i, :, x, c], r_one[j, i])
                    else:
                        gbuf[j, i, y, :, c] = plus(gbuf[j, i, y, :, c], r_one[j, i])
                two_copy(j, e).start()

        @pl.when((it >= 3) & (it < units + 3))
        def _():
            for e in (0, 1):
                j = 2 * (it - 3) + e
                two_copy(j, e).wait()
                for i in range(n):
                    gbuf[j, i, y, x, c] = plus(gbuf[j, i, y, x, c], r_two[j, i])
                for d in range(1, n):
                    z_copy(j, d).start()

        @pl.when(it >= 4)
        def _():
            for e in (0, 1):
                j = 2 * (it - 4) + e
                total = gbuf[j, me, y, x, c].astype(jnp.float32)
                for d in range(1, n):
                    z_copy(j, d).wait()
                    total = total + r_z[j, d - 1].astype(jnp.float32)
                out_ref[:, pl.ds(pl.multiple_of(j * LANE, LANE), LANE)] = total

        return carry

    lax.fori_loop(0, units + 4, turn, 0)


def scatter_sums(lefts, rights, gain_columns, edges):
    n = lax.axis_size("fsdp")
    rows = lefts.shape[1]
    r = rows // (8 * n)
    width = rights.shape[1]
    chunks = width // LANE
    half = jnp.bfloat16
    sem = pltpu.SemaphoreType.DMA
    vmem = pl.BlockSpec(memory_space=pltpu.VMEM)
    return pl.pallas_call(
        functools.partial(scatter_kernel, n, edges),
        out_shape=jax.ShapeDtypeStruct((r, width), jnp.float32),
        in_specs=[vmem] * 3,
        out_specs=vmem,
        scratch_shapes=[
            pltpu.VMEM((chunks, n, 2, 2, 2, r, LANE), half),
            pltpu.VMEM((chunks, n, 2, 2, r, LANE), half),
            pltpu.VMEM((chunks, n, 2, r, LANE), half),
            pltpu.VMEM((chunks, n, r, LANE), half),
            pltpu.VMEM((chunks, n - 1, r, LANE), half),
            sem((chunks,)),
            sem((chunks,)),
            sem((chunks,)),
            sem((chunks,)),
            sem((chunks,)),
            sem((chunks,)),
            sem((chunks, n - 1)),
            sem((chunks, n - 1)),
        ],
        compiler_params=pltpu.CompilerParams(
            collective_id=1, has_side_effects=True, vmem_limit_bytes=62 * 1024 * 1024
        ),
        name="scatter_sums",
    )(lefts, rights, gain_columns)


def padded(cells, sides, width):
    for axis, dim in sides:
        count = lax.axis_size(axis)
        ends = count - 1
        head = lax.slice_in_dim(cells, 0, width, axis=dim)
        tail = lax.slice_in_dim(cells, cells.shape[dim] - width, cells.shape[dim], axis=dim)
        cells = jnp.concatenate(
            [
                lax.ppermute(tail, axis, [(i, (i + 1) % count) for i in range(ends)]),
                cells,
                lax.ppermute(head, axis, [((i + 1) % count, i) for i in range(ends)]),
            ],
            axis=dim,
        )
    return cells


def layer_norm(values, norm_gain):
    centre = values - jnp.mean(values, axis=-1, keepdims=True)
    spread = jnp.mean(centre * centre, axis=-1, keepdims=True)
    return centre * lax.rsqrt(spread + norm_eps) * norm_gain


def rope_tables(positions, head_dim):
    half_dim = head_dim // 2
    inv_freq = rope_base ** (-(2.0 * jnp.arange(half_dim, dtype=jnp.float32)) / head_dim)
    angles = positions.astype(jnp.float32)[:, None] * inv_freq[None, :]
    return (jnp.cos(angles), jnp.sin(angles))


def rotate(values, cos_table, sin_table, head_count):
    tok_rows = values.shape[0]
    shaped = values.reshape(tok_rows, head_count, -1)
    half_dim = shaped.shape[-1] // 2
    first_half = shaped[..., :half_dim]
    second = shaped[..., half_dim:]
    cos_part = cos_table[:, None, :]
    sin_part = sin_table[:, None, :]
    turned = jnp.concatenate(
        [first_half * cos_part - second * sin_part, second * cos_part + first_half * sin_part],
        axis=-1,
    )
    return turned.reshape(tok_rows, -1)


def gated_gelu(gate, linear):
    return jax.nn.gelu(gate, approximate=False) * linear


def local(tokens, segment_ids, w_qkv, w_attn_out, w_in, w_mlp_out, norm_gains, cotangent):
    tok_rows = tokens.shape[1]
    model_width = tokens.shape[2]
    half_win = WIN // 2
    score_scale = HD ** (-0.5)
    row_start = lax.axis_index("seq") * tok_rows
    ff = w_in.shape[2]
    ff_wide = up_to(ff, 128)
    tail = up_to(ff_wide + 128, SUB) - ff_wide
    stretch = ((0, 0), (0, ff_wide - ff))
    full_qkv, full_out, full_gate, full_lin, full_down = gather_weights(
        [
            w_qkv,
            w_attn_out,
            jnp.pad(w_in[:, 0], stretch),
            jnp.pad(w_in[:, 1], stretch),
            jnp.concatenate(
                [
                    jnp.pad(w_mlp_out.T, stretch),
                    jnp.pad(norm_gains.T, ((0, 0), (0, tail - norm_gains.shape[0]))),
                ],
                axis=1,
            ),
        ]
    )
    full_mlp = full_down[:, :ff_wide]
    gain_pair = full_down[:, ff_wide : ff_wide + norm_gains.shape[0]].T.astype(jnp.float32)
    inputs = tokens[0].astype(jnp.float32)
    cos_table, sin_table = rope_tables(row_start + jnp.arange(tok_rows, dtype=jnp.int32), HD)
    h_one, norm_one_back = jax.vjp(layer_norm, inputs, gain_pair[0])
    a_one = h_one.astype(jnp.bfloat16)
    qkv_full = jnp.dot(a_one, full_qkv, preferred_element_type=jnp.float32)
    query_rows = rotate(qkv_full[:, :model_width], cos_table, sin_table, HEADS).astype(jnp.bfloat16)
    key_rows = rotate(
        qkv_full[:, model_width : 2 * model_width], cos_table, sin_table, HEADS
    ).astype(jnp.bfloat16)
    value_rows = qkv_full[:, 2 * model_width :].astype(jnp.bfloat16)
    kv_wide = padded(jnp.concatenate([key_rows, value_rows], axis=1), (("seq", 0),), half_win)
    key_wide = kv_wide[:, :model_width].reshape(-1, HEADS, HD)
    value_wide = kv_wide[:, model_width:].reshape(-1, HEADS, HD)
    row_ids = segment_ids[0]
    ids_pad = jnp.pad(row_ids, (half_win, half_win), constant_values=-1)
    k_ids = lax.dynamic_slice_in_dim(ids_pad, row_start, tok_rows + 2 * half_win)
    q_ids = lax.dynamic_slice_in_dim(row_ids, row_start, tok_rows)
    offsets = (
        jnp.arange(tok_rows)[:, None] - jnp.arange(tok_rows + 2 * half_win)[None, :] + half_win
    )
    allowed = (jnp.abs(offsets) <= half_win) & (q_ids[:, None] == k_ids[None, :])
    q_heads = query_rows.reshape(tok_rows, HEADS, HD)
    scores = (
        jnp.einsum("thd,shd->hts", q_heads, key_wide, preferred_element_type=jnp.float32)
        * score_scale
    )
    scores = jnp.where(allowed[None], scores, masked_score)
    row_max = jnp.max(scores, axis=-1, keepdims=True)
    exponent = jnp.exp(scores - row_max)
    row_sum = jnp.sum(exponent, axis=-1, keepdims=True)
    attn_p = exponent / row_sum
    attn_pb = attn_p.astype(jnp.bfloat16)
    attn_o = jnp.einsum("hts,shd->thd", attn_pb, value_wide, preferred_element_type=jnp.float32)
    attn_ob = attn_o.reshape(tok_rows, model_width).astype(jnp.bfloat16)
    residual = inputs + jnp.dot(attn_ob, full_out, preferred_element_type=jnp.float32)
    h_two, norm_two_back = jax.vjp(layer_norm, residual, gain_pair[1])
    a_two = h_two.astype(jnp.bfloat16)
    gate = jnp.dot(a_two, full_gate, preferred_element_type=jnp.float32)
    linear = jnp.dot(a_two, full_lin, preferred_element_type=jnp.float32)
    middle, gelu_back = jax.vjp(gated_gelu, gate, linear)
    middle_b = middle.astype(jnp.bfloat16)
    outputs = (
        residual + jnp.einsum("tf,df->td", middle_b, full_mlp, preferred_element_type=jnp.float32)
    ).astype(
        jnp.bfloat16
    )
    back_qkv, back_out = (full_qkv, full_out)
    grad_out = cotangent[0].astype(jnp.float32)
    grad_mlp_b = grad_out.astype(jnp.bfloat16)
    grad_mid = jnp.dot(grad_mlp_b, full_mlp, preferred_element_type=jnp.float32)
    grad_gate_b, grad_lin_b = [g.astype(jnp.bfloat16) for g in gelu_back(grad_mid)]
    grad_a_two = jnp.einsum(
        "tf,df->td", grad_gate_b, full_gate, preferred_element_type=jnp.float32
    ) + jnp.einsum("tf,df->td", grad_lin_b, full_lin, preferred_element_type=jnp.float32)
    grad_res_norm, grad_gain_two = norm_two_back(grad_a_two)
    grad_res = grad_out + grad_res_norm
    grad_att_b = grad_res.astype(jnp.bfloat16)
    grad_o_b = jnp.einsum(
        "te,de->td", grad_att_b, back_out, preferred_element_type=jnp.float32
    ).astype(jnp.bfloat16)
    grad_o_heads = grad_o_b.reshape(tok_rows, HEADS, HD)
    grad_prob = jnp.einsum(
        "thd,shd->hts", grad_o_heads, value_wide, preferred_element_type=jnp.float32
    )
    delta_sum = jnp.sum(grad_prob * attn_p, axis=-1, keepdims=True)
    grad_scores_b = (attn_p * (grad_prob - delta_sum)).astype(jnp.bfloat16)
    grad_query = (
        jnp.einsum("hts,shd->thd", grad_scores_b, key_wide, preferred_element_type=jnp.float32)
        * score_scale
    )
    grad_key_wide = (
        jnp.einsum("hts,thd->shd", grad_scores_b, q_heads, preferred_element_type=jnp.float32)
        * score_scale
    )
    grad_value_wide = jnp.einsum(
        "hts,thd->shd", attn_pb, grad_o_heads, preferred_element_type=jnp.float32
    )
    grad_kv_wide = jnp.concatenate(
        [grad_key_wide.reshape(-1, model_width), grad_value_wide.reshape(-1, model_width)], axis=1
    )
    rim_grads = jnp.concatenate(
        [grad_kv_wide[:half_win], grad_kv_wide[tok_rows + half_win :]], axis=0
    )
    arrived = padded(rim_grads.astype(jnp.bfloat16), (("seq", 0),), half_win).astype(
        rim_grads.dtype
    )
    own_grads = grad_kv_wide[half_win : half_win + tok_rows]
    own_grads = own_grads + jnp.pad(arrived[:half_win], ((0, tok_rows - half_win), (0, 0)))
    own_grads = own_grads + jnp.pad(arrived[3 * half_win :], ((tok_rows - half_win, 0), (0, 0)))
    grad_qkv_b = jnp.concatenate(
        [
            rotate(grad_query.reshape(tok_rows, model_width), cos_table, -sin_table, HEADS),
            rotate(own_grads[:, :model_width], cos_table, -sin_table, HEADS),
            own_grads[:, model_width:],
        ],
        axis=1,
    ).astype(jnp.bfloat16)
    grad_a_one = jnp.einsum("te,de->td", grad_qkv_b, back_qkv, preferred_element_type=jnp.float32)
    grad_in_norm, grad_gain_one = norm_one_back(grad_a_one)
    input_grad = grad_res + grad_in_norm
    gains_cols = jnp.stack([grad_gain_one, grad_gain_two], axis=1)
    shares = lax.axis_size("fsdp") * lax.axis_size("seq")
    lefts = [a_one, attn_ob, a_two, grad_mlp_b]
    widths = [3 * model_width, model_width, 2 * ff_wide, ff_wide]
    rights = [
        grad_qkv_b,
        grad_att_b,
        jnp.concatenate([grad_gate_b, grad_lin_b], axis=1),
        middle_b,
    ]
    total_width = sum(widths) + tail
    fits = (
        lax.axis_size("seq") == 8
        and model_width % (16 * shares) == 0
        and total_width % (2 * LANE) == 0
        and all(w % SUB == 0 for w in widths[:3])
    )
    if fits:
        edges = [sum(widths[: i + 1]) // SUB for i in range(3)]
        summed = scatter_sums(
            jnp.stack([left.T for left in lefts]),
            jnp.concatenate(rights + [jnp.zeros((tok_rows, tail), jnp.bfloat16)], axis=1),
            jnp.pad(gains_cols, ((0, 0), (0, 128 - gains_cols.shape[1]))).astype(jnp.bfloat16),
            edges,
        )
        gains_at = total_width - 128
    else:
        summed = lax.psum_scatter(
            jnp.concatenate(
                [
                    jnp.einsum("td,te->de", left, right, preferred_element_type=jnp.float32)
                    for left, right in zip(lefts, rights)
                ]
                + [gains_cols],
                axis=1,
            ),
            ("fsdp", "seq"),
            scatter_dimension=0,
            tiled=True,
        )
        gains_at = sum(widths)
    edge_one = widths[0]
    edge_two = edge_one + widths[1]
    edge_three = edge_two + widths[2]
    sum_qkv = summed[:, :edge_one]
    sum_out = summed[:, edge_one:edge_two]
    sum_in = jnp.stack(
        [summed[:, edge_two : edge_two + ff], summed[:, edge_two + ff_wide : edge_two + ff_wide + ff]],
        axis=1,
    )
    sum_mlp = summed[:, edge_three : edge_three + ff].T
    sum_gains = summed[:, gains_at : gains_at + 2].T
    return (outputs[None], input_grad[None], sum_qkv, sum_out, sum_in, sum_mlp, sum_gains)


def solution(mesh):
    return jax.shard_map(
        local,
        mesh=mesh,
        in_specs=(
            P("fsdp", "seq", None),
            P("fsdp", None),
            P("fsdp", None),
            P("fsdp", None),
            P("fsdp", None, None),
            P(None, "fsdp"),
            P(None, "fsdp"),
            P("fsdp", "seq", None),
        ),
        out_specs=(
            P("fsdp", "seq", None),
            P("fsdp", "seq", None),
            P(("fsdp", "seq"), None),
            P(("fsdp", "seq"), None),
            P(("fsdp", "seq"), None, None),
            P(None, ("fsdp", "seq")),
            P(None, ("fsdp", "seq")),
        ),
        check_vma=False,
    )
```
